256 devices in a mesh: row: 8 (over y, z_lo), col: 32 (over z_hi, x, core).
Axes of the slice: x: 4, y: 4, z: 8 (z_hi: 4, z_lo: 2; z = z_hi * 2 + z_lo), core: 2. Of those that a mesh axis runs over, the one named last changes fastest.
Arguments:
- blocks: float32 [8192, 128, 128], P(('row', 'col')), may hold values from -0.21875 to 0.21875
- block_row: int32 [8192], P(('row', 'col')), may hold values from 0 to 511, as said below
- block_col: int32 [8192], P(('row', 'col')), may hold values from 0 to 511, as said below
- counts: int32 [256], P(('row', 'col')), may hold values from 1 to 32, as said below
- diagonal: float32 [65536], P(('row', 'col')), may hold values from 0.25 to 4
- vector: float32 [65536, 256], P(('row', 'col')), may hold values from -8 to 8
Outputs:
- next_basis: float32 [65536, 256], P(('row', 'col'))
- second_image: float32 [65536, 256], P(('row', 'col'))
- arnoldi_column: float32 [2, 256], replicated
The draws below stay inside these ranges and needn't reach their ends.
Inputs may be any that keep to these rules, and one draw needn't show every extreme that they name: The slots of device d = r * 32 + c are rows d * 32 to (d + 1) * 32 - 1. Its slot d * 32 + k * 32 + o (k below 1) has block_row // 2 equal to r * 32 + o, and (block_col // 2) % 32 equals c. No pair (block_row, block_col) occurs twice among all slots. `block_col`: paired with block_row as stated there. Only the first counts[d] slots of device d hold blocks; later slots are ignored. Some device has exactly 32.
All inputs are finite; a program needn't handle non-finite values.
Results may differ from the reference program's by a relative error of at most 0.0001.
Values sent between devices are 32-bit elements; how exact they have to be, the bound alone decides.
No kernel may reach another device: no remote copies, remote signals or barrier semaphores. Data moves between devices by JAX's collectives and lax.ppermute only.
A program may use at most 64 MiB of HBM per device.

```python
import math
import jax
import jax.numpy as jnp
from jax import lax

BLK = 128
VB = 2
CAP = 1
RHS = 256
MAXB = 32
NV = 65536
N_ROW = 8
N_COL = 32


def positions_of(key):
    device_count = N_ROW * N_COL
    choices_each = VB * N_ROW * VB
    keys = jax.random.split(jax.random.fold_in(key, 11), device_count * N_COL)

    def one_list(single):
        return jax.random.permutation(single, choices_each).astype(jnp.int32)[:CAP]
    spots = jax.vmap(one_list)(keys).astype(jnp.int32).reshape(device_count, N_COL, CAP)
    spots = jnp.transpose(spots, (0, 2, 1)).reshape(device_count, CAP * N_COL)
    device_ids = jnp.arange(device_count, dtype=jnp.int32)[:, None]
    grid_row = device_ids // N_COL
    grid_col = device_ids % N_COL
    target_col = (jnp.arange(CAP * N_COL, dtype=jnp.int32) % N_COL)[None, :]
    local_row = spots // (N_ROW * VB)
    local_col = spots % (N_ROW * VB)
    global_row = (grid_row * N_COL + target_col) * VB + local_row
    global_col = (local_col // VB * N_COL + grid_col) * VB + local_col % VB
    return (global_row.reshape(-1).astype(jnp.int32), global_col.reshape(-1).astype(jnp.int32))


def draw_block_row(key, part):
    return positions_of(key)[0]


def draw_block_col(key, part):
    return positions_of(key)[1]


def draw_counts(key, part):
    device_count = N_ROW * N_COL
    first_key, second_key, third_key = jax.random.split(jax.random.fold_in(key, 5), 3)
    exponent = jax.random.randint(first_key, (device_count,), 0, 4)
    base_count = MAXB // jnp.left_shift(jnp.ones((device_count,), jnp.int32), exponent)
    reduction = jax.random.randint(second_key, (device_count,), 0, base_count // 2 + 1)
    chosen = jnp.maximum(base_count - reduction, 1)
    busiest = jax.random.randint(third_key, (), 0, device_count)
    return jnp.where(jnp.arange(device_count) == busiest, MAXB, chosen).astype(jnp.int32)


def draw_vector(key, part):
    first_key = jax.random.fold_in(jax.random.fold_in(key, 3), 0)
    ramp = 0.6 + 1.2 * jnp.arange(NV, dtype=jnp.float32)[:, None] / NV
    values = jnp.clip(jax.random.normal(first_key, (NV, RHS), jnp.float32), -4.0, 4.0)
    return (values * ramp).astype(jnp.float32)


def steps_of(own_key, dims, pieces, low, high):
    loudness, own = 1.0, jax.random.fold_in(own_key, 6)
    for axis_at, blocks in pieces:
        draws = jnp.exp(jax.random.uniform(jax.random.fold_in(own, axis_at), (blocks,), jnp.float32, low / len(pieces), high / len(pieces)))
        loudness = loudness * jnp.repeat(draws, dims[axis_at] // blocks).reshape([-1 if axis == axis_at else 1 for axis in range(len(dims))])
    return loudness


def noise(rng, extent, width, bound, pieces=(), kind=jnp.bfloat16):
    array = width * jax.random.normal(rng, extent, jnp.float32)
    if pieces:
        array = array * steps_of(rng, extent, pieces, -0.22, 0.18)
    return jnp.clip(array, -bound, bound).astype(kind)


def setup_inputs(seed: int = 0) -> dict:
    streams_of = jax.random.split(jax.random.key(seed), 7)
    blocks = noise(streams_of[0], (N_ROW * N_COL * MAXB, BLK, BLK), (BLK * MAXB // (3 * VB)) ** -0.5, 0.21875, ((0, 256),), jnp.float32)
    block_row = draw_block_row(jax.random.fold_in(streams_of[6], 71), 0)
    block_col = draw_block_col(jax.random.fold_in(streams_of[6], 71), 0)
    counts = draw_counts(jax.random.fold_in(streams_of[6], 71), 0)
    diagonal = jnp.clip(jnp.exp(math.log(4.0) - 2.7725887 * jax.random.uniform(streams_of[4], (NV,), jnp.float32) ** steps_of(streams_of[4], (NV,), ((0, 256),), -0.2, 0.2)), 0.25, 4.0)
    vector = draw_vector(jax.random.fold_in(streams_of[6], 71), 0)
    return dict(blocks=blocks, block_row=block_row, block_col=block_col, counts=counts, diagonal=diagonal, vector=vector)


def apply_transpose(source, diagonal, blocks, block_row, block_col, counts):
    device_count = counts.shape[0]
    tile_size = blocks.shape[1]
    slot_count = blocks.shape[0] // device_count
    rhs_count = source.shape[1]
    block_total = source.shape[0] // tile_size
    stacked = source.reshape(block_total, tile_size, rhs_count)
    live_slot = (jnp.arange(slot_count, dtype=jnp.int32)[None, :] < counts[:, None]).astype(jnp.float32)

    def advance(totals, inputs):
        tile_set, row_ids, col_ids, weights = inputs
        picked = stacked[row_ids]
        products = jnp.einsum('mab,mak->mbk', tile_set, picked, precision=lax.Precision.HIGHEST)
        products = products * weights[:, None, None]
        return (totals.at[col_ids].add(products), None)
    start_sum = jnp.zeros((block_total, tile_size, rhs_count), jnp.float32)
    totals, _ = lax.scan(advance, start_sum, (blocks.reshape(device_count, slot_count, tile_size, tile_size), block_row.reshape(device_count, slot_count), block_col.reshape(device_count, slot_count), live_slot))
    return diagonal[:, None] * source + totals.reshape(source.shape)

def reference(blocks, block_row, block_col, counts, diagonal, vector):
    magnitude = jnp.sqrt(lax.optimization_barrier(jnp.mean(vector * vector, axis=0)) + 1e-06)
    unit_basis = vector / magnitude
    first_image = apply_transpose(unit_basis, diagonal, blocks, block_row, block_col, counts)
    projection = lax.optimization_barrier(jnp.mean(first_image * unit_basis, axis=0))
    remainder = first_image - projection * unit_basis
    norm_new = jnp.sqrt(lax.optimization_barrier(jnp.mean(remainder * remainder, axis=0)) + 1e-06)
    next_basis = remainder / norm_new
    second_image = apply_transpose(next_basis, diagonal, blocks, block_row, block_col, counts)
    return (next_basis, second_image, jnp.stack([projection, norm_new]))
```

```python
import functools

import jax
import jax.numpy as jnp
from jax import lax
from jax.experimental import pallas as pl
from jax.experimental.pallas import tpu as pltpu
from jax.sharding import PartitionSpec as P

TILE = 128
HALF = 128
STAT = 8
LIMIT = 48 * 1024 * 1024
OFFSETS = (0, 3, 1, 2)


def col_index(z, x, core):
    return (z % 4) * 8 + (x % 4) * 2 + core


def col_pairs(dz, dx):
    return [
        (col_index(z, x, k), col_index(z + dz, x + dx, k))
        for z in range(4)
        for x in range(4)
        for k in range(2)
    ]


def smem():
    return pl.BlockSpec(memory_space=pltpu.SMEM)


def vmem():
    return pl.BlockSpec(memory_space=pltpu.VMEM)


def params():
    return pltpu.CompilerParams(vmem_limit_bytes=LIMIT)


def split_blocks_kernel(counts, blocks, out):
    base = pl.program_id(0) * blocks.shape[0]
    for i in range(blocks.shape[0]):
        block = jnp.where(base + i < counts[0], blocks[i], 0.0).T
        high = block.astype(jnp.bfloat16)
        low = (block - high.astype(jnp.float32)).astype(jnp.bfloat16)
        out[i, :, :TILE] = high
        out[i, :, TILE:] = low


def split_blocks(counts, blocks):
    n, step = blocks.shape[0], 8
    return pl.pallas_call(
        split_blocks_kernel,
        grid=(n // step,),
        out_shape=jax.ShapeDtypeStruct((n, TILE, 2 * TILE), jnp.bfloat16),
        in_specs=[smem(), pl.BlockSpec((step, TILE, TILE), lambda i: (i, 0, 0))],
        out_specs=pl.BlockSpec((step, TILE, 2 * TILE), lambda i: (i, 0, 0)),
        compiler_params=params(),
        name="split_blocks",
    )(counts, blocks)


def pieces_of(near, left, right, far_top, far_bottom):
    listed = []
    for dx, ref in ((0, near), (3, left), (1, right)):
        listed += [(dx, dz, ref, i) for i, dz in enumerate(OFFSETS)]
    listed += [(2, dz, far_top, i) for i, dz in enumerate(OFFSETS[:2])]
    listed += [(2, dz, far_bottom, i) for i, dz in enumerate(OFFSETS[2:])]
    return listed


def slot_of(place, dx, dz, core):
    return ((place[0] + dz) & 3) * 8 + ((place[1] + dx) & 3) * 2 + core


def pick_kernel(place, rows, near, left, right, far_top, far_bottom, out):
    for n, (dx, dz, ref, i) in enumerate(pieces_of(near, left, right, far_top, far_bottom)):
        slot = slot_of(place, dx, dz, place[2])
        start = pl.multiple_of((rows[slot] & 1) * TILE, TILE)
        out[n, :TILE] = ref[i, pl.ds(start, TILE)]
        if out.shape[1] > TILE:
            out[n, TILE:] = ref[i, 2 * TILE :]


def pick_for_partner(place, partner_rows, gathered):
    extra = gathered[0].shape[1] - 2 * TILE
    return pl.pallas_call(
        pick_kernel,
        out_shape=jax.ShapeDtypeStruct((16, TILE + extra, HALF), jnp.float32),
        in_specs=[smem(), smem()] + [vmem()] * 5,
        out_specs=vmem(),
        compiler_params=params(),
        name="pick_for_partner",
    )(place, partner_rows, *gathered)


def merge(stats):
    squares, inner, rest = stats
    ratio = jnp.where(squares > 0, inner / jnp.where(squares > 0, squares, 1.0), 0.0)
    total, inner_total = jnp.sum(squares, axis=0), jnp.sum(inner, axis=0)
    safe = jnp.where(total > 0, total, 1.0)
    mean_ratio = jnp.where(total > 0, inner_total / safe, 0.0)
    away = ratio - mean_ratio[None]
    return total, inner_total, jnp.sum(rest + squares * away * away, axis=0), mean_ratio


def multiply_kernel(place, rows, cols, split, near, left, right, far_top, far_bottom, other, out, *stats):
    out[...] = jnp.zeros_like(out)
    with_stats = out.shape[1] > 2 * TILE
    core = place[2]

    def add(slot, source):
        high = source.astype(jnp.bfloat16)
        low = (source - high.astype(jnp.float32)).astype(jnp.bfloat16)
        row = jnp.concatenate([high, low], axis=1)
        wide = jnp.dot(
            split[slot],
            jnp.concatenate([row, row], axis=0),
            preferred_element_type=jnp.float32,
        )
        target = cols[slot]
        owner = lax.shift_right_logical(target, 6)
        start = pl.multiple_of((target & 1) * TILE, TILE)
        out[owner, pl.ds(start, TILE)] += wide[:, :HALF] + wide[:, HALF:]

    for n, (dx, dz, ref, i) in enumerate(pieces_of(near, left, right, far_top, far_bottom)):
        slot = slot_of(place, dx, dz, core)
        start = pl.multiple_of((rows[slot] & 1) * TILE, TILE)
        add(slot, ref[i, pl.ds(start, TILE)])
        slot_other = slot_of(place, dx, dz, 1 - core)
        add(slot_other, other[n, :TILE])
        if with_stats:
            stats[0][slot] = ref[i, 2 * TILE :]
            stats[0][slot_other] = other[n, TILE:]
    if with_stats:
        total, inner, rest, _ = merge([stats[0][:, k : k + 1, :] for k in range(3)])
        joined = jnp.concatenate([total, inner, rest, jnp.zeros((STAT - 3, HALF), jnp.float32)], axis=0)
        for owner in range(out.shape[0]):
            out[owner, 2 * TILE :] = joined


def multiply(place, rows, cols, split, gathered, other):
    height = gathered[0].shape[1]
    return pl.pallas_call(
        multiply_kernel,
        out_shape=jax.ShapeDtypeStruct((8, height, HALF), jnp.float32),
        in_specs=[smem()] * 3 + [vmem()] * 7,
        out_specs=vmem(),
        scratch_shapes=[pltpu.VMEM((32, STAT, HALF), jnp.float32)] if height > 2 * TILE else [],
        compiler_params=params(),
        name="multiply",
    )(place, rows, cols, split, *gathered, other)


def sum_terms(terms, diagonal, source):
    total = terms[0, : 2 * TILE]
    for k in range(1, terms.shape[0]):
        total = total + terms[k, : 2 * TILE]
    return diagonal[...] * source + total


def first_image_kernel(terms, diagonal, vector, out):
    v = vector[...]
    w = sum_terms(terms, diagonal, v)
    out[: 2 * TILE] = w
    squares = jnp.sum(v * v, axis=0, keepdims=True)
    inner = jnp.sum(w * v, axis=0, keepdims=True)
    ratio = jnp.where(squares > 0, inner / jnp.where(squares > 0, squares, 1.0), 0.0)
    away = w - ratio * v
    rest = jnp.sum(away * away, axis=0, keepdims=True)
    out[2 * TILE :] = jnp.concatenate(
        [squares, inner, rest, jnp.zeros((STAT - 3, HALF), jnp.float32)], axis=0
    )


def first_image(terms, diagonal, vector):
    return pl.pallas_call(
        first_image_kernel,
        out_shape=jax.ShapeDtypeStruct((2 * TILE + STAT, HALF), jnp.float32),
        in_specs=[vmem()] * 3,
        out_specs=vmem(),
        compiler_params=params(),
        name="first_image",
    )(terms, diagonal, vector)


def finish_kernel(count, diagonal, *refs):
    (terms_a, image_a, vector_a, terms_b, image_b, vector_b, basis, second, column) = refs
    for half, (terms, image, vector) in enumerate(
        ((terms_a, image_a, vector_a), (terms_b, image_b, vector_b))
    ):
        span = slice(half * HALF, (half + 1) * HALF)
        stats = [terms[:, 2 * TILE + k : 2 * TILE + k + 1, :] for k in range(3)]
        squares, inner, rest, ratio = merge(stats)
        mean = squares / count + 1e-06
        magnitude = jnp.sqrt(mean)
        projection = inner / count / mean
        gap = projection - ratio
        left_over = rest + squares * gap * gap
        norm = jnp.sqrt(left_over / count / mean + 1e-06)
        column[0:1, span] = projection
        column[1:2, span] = norm
        w = image[: 2 * TILE]
        scale = 1.0 / (magnitude * norm)
        basis[:, span] = (w - projection * vector[...]) * scale
        second[:, span] = (sum_terms(terms, diagonal, w) - projection * w) * scale


def finish(count, diagonal, halves):
    flat = [part for half in halves for part in half]
    return pl.pallas_call(
        functools.partial(finish_kernel, count),
        out_shape=(
            jax.ShapeDtypeStruct((2 * TILE, 2 * HALF), jnp.float32),
            jax.ShapeDtypeStruct((2 * TILE, 2 * HALF), jnp.float32),
            jax.ShapeDtypeStruct((2, 2 * HALF), jnp.float32),
        ),
        in_specs=[vmem()] * 7,
        out_specs=(vmem(),) * 3,
        compiler_params=params(),
        name="finish",
    )(diagonal, *flat)


def ring_gather(own, pairs):
    send = lambda part, step: lax.ppermute(part, "col", pairs(step))
    n = own.shape[0]
    back, ahead = send(own, 1), send(own, 3)
    if n == 1:
        cut = TILE
        far = jnp.concatenate(
            [send(back[:, :cut], 1), send(ahead[:, cut:], 3)], axis=1
        )
        return own, back, ahead, far
    return own, back, ahead, send(back[: n // 2], 1), send(ahead[n // 2 :], 3)


def gather_z(own):
    return jnp.concatenate(ring_gather(own[None], lambda step: col_pairs(step, 0)), axis=0)


def gather_x(stack):
    return ring_gather(stack, lambda step: col_pairs(0, step))


def swap_cores(part):
    return lax.ppermute(part, "col", [(i, i ^ 1) for i in range(32)])


def per_device(blocks, block_row, block_col, counts, diagonal, vector):
    count = vector.shape[0] * lax.axis_size("row") * lax.axis_size("col")
    index = lax.axis_index("col")
    place = jnp.stack([index // 8, index // 2 % 4, index % 2]).astype(jnp.int32)
    partner_rows = swap_cores(block_row)
    vectors = [vector[:, :HALF], vector[:, HALF:]]
    diagonal = jnp.broadcast_to(diagonal[:, None], (2 * TILE, HALF))

    def product(sources):
        stacks = [gather_z(source) for source in sources]
        gathered = [gather_x(stack) for stack in stacks]
        terms = []
        for each in gathered:
            other = swap_cores(pick_for_partner(place, partner_rows, each))
            partial = multiply(place, block_row, block_col, split, each, other)
            terms.append(lax.all_to_all(partial, "row", 0, 0, tiled=True))
        return terms

    split = split_blocks(counts, blocks)
    terms = product(vectors)
    images = [first_image(t, diagonal, v) for t, v in zip(terms, vectors)]
    terms = product(images)
    return finish(count, diagonal, list(zip(terms, images, vectors)))


def solution(mesh):
    return jax.shard_map(
        per_device,
        mesh=mesh,
        in_specs=(
            P(("row", "col"), None, None),
            P(("row", "col")),
            P(("row", "col")),
            P(("row", "col")),
            P(("row", "col")),
            P(("row", "col"), None),
        ),
        out_specs=(P(("row", "col"), None), P(("row", "col"), None), P()),
        check_vma=False,
    )
```

```python
import functools

import jax
import jax.numpy as jnp
from jax import lax
from jax.experimental import pallas as pl
from jax.experimental.pallas import tpu as pltpu
from jax.sharding import PartitionSpec as P

TILE = 128
WIDTH = 256
STAT = 8
LIMIT = 48 * 1024 * 1024


def col_index(z, x, core):
    return (z % 4) * 8 + (x % 4) * 2 + core


def col_pairs(along_z):
    pairs = []
    for z in range(4):
        for x in range(4):
            for core, step in ((0, 1), (1, 3)):
                to = (z + step, x) if along_z else (z, x + step)
                pairs.append((col_index(z, x, core), col_index(*to, core)))
    return pairs


def smem():
    return pl.BlockSpec(memory_space=pltpu.SMEM)


def vmem():
    return pl.BlockSpec(memory_space=pltpu.VMEM)


def params():
    return pltpu.CompilerParams(vmem_limit_bytes=LIMIT)


def split_blocks_kernel(counts, blocks, out):
    base = pl.program_id(0) * blocks.shape[0]
    for i in range(blocks.shape[0]):
        block = jnp.where(base + i < counts[0], blocks[i], 0.0).T
        high = block.astype(jnp.bfloat16)
        low = (block - high.astype(jnp.float32)).astype(jnp.bfloat16)
        out[i, :, :TILE] = high
        out[i, :, TILE:] = low


def split_blocks(counts, blocks):
    n, step = blocks.shape[0], 8
    return pl.pallas_call(
        split_blocks_kernel,
        grid=(n // step,),
        out_shape=jax.ShapeDtypeStruct((n, TILE, 2 * TILE), jnp.bfloat16),
        in_specs=[smem(), pl.BlockSpec((step, TILE, TILE), lambda i: (i, 0, 0))],
        out_specs=pl.BlockSpec((step, TILE, 2 * TILE), lambda i: (i, 0, 0)),
        compiler_params=params(),
        name="split_blocks",
    )(counts, blocks)


NONE, WAY, AGAINST, TWO = range(4)
CHIP = ((NONE, 1), (NONE, 0))
MID = ((WAY, 1), (WAY, 0), (AGAINST, 0), (AGAINST, 1))
LAST = ((TWO, 1), (TWO, 0))


def named(dx, keys, ref):
    return [(dx, *key, ref, i) for i, key in enumerate(keys)]


def early_pieces(chip, mid, last):
    return named(NONE, CHIP, chip) + named(NONE, MID, mid) + named(NONE, LAST, last)


def early_brought(chip, mid, last, far):
    return named(WAY, CHIP, chip) + named(WAY, MID, mid) + named(WAY, LAST, last) + named(TWO, CHIP[1:], far)


def late_brought(mid, last):
    return named(TWO, MID[:2], mid) + named(TWO, LAST[1:], last)


def slot_of(place, dx, dz, other, core):
    steps = (0, 3 - 2 * core, 1 + 2 * core, 2)
    number = 1 - core if other else core
    return ((place[0] + steps[dz]) & 3) * 8 + ((place[1] + steps[dx]) & 3) * 2 + number


def pick_kernel(layout, place, rows, *refs):
    *brought, out = refs
    for n, (dx, dz, other, ref, i) in enumerate(layout(*brought)):
        slot = slot_of(place, dx, dz, other, place[2])
        start = pl.multiple_of((rows[slot] & 1) * TILE, TILE)
        out[n, :TILE] = ref[i, pl.ds(start, TILE)]
        if out.shape[1] > TILE:
            out[n, TILE:] = ref[i, 2 * TILE :]


def pick_for_partner(layout, place, partner_rows, brought):
    extra = brought[0].shape[1] - 2 * TILE
    return pl.pallas_call(
        functools.partial(pick_kernel, layout),
        out_shape=jax.ShapeDtypeStruct((len(layout(*brought)), TILE + extra, WIDTH), jnp.float32),
        in_specs=[smem(), smem()] + [vmem()] * len(brought),
        out_specs=vmem(),
        compiler_params=params(),
        name="pick_for_partner",
    )(place, partner_rows, *brought)


def merge(stats):
    squares, inner, rest = stats
    ratio = jnp.where(squares > 0, inner / jnp.where(squares > 0, squares, 1.0), 0.0)
    total, inner_total = jnp.sum(squares, axis=0), jnp.sum(inner, axis=0)
    safe = jnp.where(total > 0, total, 1.0)
    mean_ratio = jnp.where(total > 0, inner_total / safe, 0.0)
    away = ratio - mean_ratio[None]
    return total, inner_total, jnp.sum(rest + squares * away * away, axis=0), mean_ratio


def add_products(place, rows, cols, split, own, brought, other, out, stats):
    core = place[2]

    def add(slot, source):
        high = source.astype(jnp.bfloat16)
        low = (source - high.astype(jnp.float32)).astype(jnp.bfloat16)
        both = split[slot]
        total = jnp.dot(
            both, jnp.concatenate([high, high], axis=0), preferred_element_type=jnp.float32
        ) + jnp.dot(both, jnp.concatenate([low, low], axis=0), preferred_element_type=jnp.float32)
        target = cols[slot]
        owner = lax.shift_right_logical(target, 6)
        start = pl.multiple_of((target & 1) * TILE, TILE)
        out[owner, pl.ds(start, TILE)] += total

    for dx, dz, foreign, ref, i in own + brought:
        slot = slot_of(place, dx, dz, foreign, core)
        start = pl.multiple_of((rows[slot] & 1) * TILE, TILE)
        add(slot, ref[i, pl.ds(start, TILE)])
        if stats is not None:
            stats[slot] = ref[i, 2 * TILE :]
    for n, (dx, dz, foreign, _, _) in enumerate(brought):
        slot = slot_of(place, dx, dz, foreign, 1 - core)
        add(slot, other[n, :TILE])
        if stats is not None:
            stats[slot] = other[n, TILE:]


def early_kernel(place, rows, cols, split, *refs):
    out, stats = refs[8], refs[9] if len(refs) > 9 else None
    out[...] = jnp.zeros_like(out)
    if stats is not None:
        stats[...] = jnp.zeros_like(stats)
    own, brought = early_pieces(*refs[:3]), early_brought(*refs[3:7])
    add_products(place, rows, cols, split, own, brought, refs[7], out, stats)


def multiply_early(place, rows, cols, split, gathered, other):
    height = gathered[0].shape[1]
    shapes = [jax.ShapeDtypeStruct((8, height, WIDTH), jnp.float32)]
    if height > 2 * TILE:
        shapes.append(jax.ShapeDtypeStruct((32, STAT, WIDTH), jnp.float32))
    return pl.pallas_call(
        early_kernel,
        out_shape=shapes,
        in_specs=[smem()] * 3 + [vmem()] * (2 + len(gathered)),
        out_specs=[vmem()] * len(shapes),
        compiler_params=params(),
        name="multiply_early",
    )(place, rows, cols, split, *gathered, other)


def late_kernel(place, rows, cols, split, mid, last, other, sums, *refs):
    if len(refs) == 1:
        out, stats = refs[0], None
    else:
        known, out, stats = refs
        stats[...] = known[...]
    out[...] = sums[...]
    add_products(place, rows, cols, split, [], late_brought(mid, last), other, out, stats)
    if stats is not None:
        total, inner, rest, _ = merge([stats[:, k : k + 1, :] for k in range(3)])
        joined = jnp.concatenate([total, inner, rest, jnp.zeros((STAT - 3, WIDTH), jnp.float32)], axis=0)
        for owner in range(out.shape[0]):
            out[owner, 2 * TILE :] = joined


def multiply_late(place, rows, cols, split, gathered, other, sums, *stats):
    return pl.pallas_call(
        late_kernel,
        out_shape=jax.ShapeDtypeStruct(sums.shape, jnp.float32),
        in_specs=[smem()] * 3 + [vmem()] * (5 + len(stats)),
        out_specs=vmem(),
        scratch_shapes=[pltpu.VMEM(each.shape, jnp.float32) for each in stats],
        compiler_params=params(),
        name="multiply_late",
    )(place, rows, cols, split, *gathered, other, sums, *stats)


def sum_terms(terms, diagonal, source):
    total = terms[0, : 2 * TILE]
    for k in range(1, terms.shape[0]):
        total = total + terms[k, : 2 * TILE]
    return diagonal[...] * source + total


def first_image_kernel(terms, diagonal, vector, out):
    v = vector[...]
    w = sum_terms(terms, diagonal, v)
    out[: 2 * TILE] = w
    squares = jnp.sum(v * v, axis=0, keepdims=True)
    inner = jnp.sum(w * v, axis=0, keepdims=True)
    ratio = jnp.where(squares > 0, inner / jnp.where(squares > 0, squares, 1.0), 0.0)
    away = w - ratio * v
    rest = jnp.sum(away * away, axis=0, keepdims=True)
    out[2 * TILE :] = jnp.concatenate(
        [squares, inner, rest, jnp.zeros((STAT - 3, WIDTH), jnp.float32)], axis=0
    )


def first_image(terms, diagonal, vector):
    return pl.pallas_call(
        first_image_kernel,
        out_shape=jax.ShapeDtypeStruct((2 * TILE + STAT, WIDTH), jnp.float32),
        in_specs=[vmem()] * 3,
        out_specs=vmem(),
        compiler_params=params(),
        name="first_image",
    )(terms, diagonal, vector)


def finish_kernel(count, diagonal, terms, image, vector, basis, second, column):
    stats = [terms[:, 2 * TILE + k : 2 * TILE + k + 1, :] for k in range(3)]
    squares, inner, rest, ratio = merge(stats)
    mean = squares / count + 1e-06
    magnitude = jnp.sqrt(mean)
    projection = inner / count / mean
    gap = projection - ratio
    left_over = rest + squares * gap * gap
    norm = jnp.sqrt(left_over / count / mean + 1e-06)
    column[0:1] = projection
    column[1:2] = norm
    w = image[: 2 * TILE]
    scale = 1.0 / (magnitude * norm)
    basis[...] = (w - projection * vector[...]) * scale
    second[...] = (sum_terms(terms, diagonal, w) - projection * w) * scale


def finish(count, diagonal, terms, image, vector):
    return pl.pallas_call(
        functools.partial(finish_kernel, count),
        out_shape=(
            jax.ShapeDtypeStruct((2 * TILE, WIDTH), jnp.float32),
            jax.ShapeDtypeStruct((2 * TILE, WIDTH), jnp.float32),
            jax.ShapeDtypeStruct((2, WIDTH), jnp.float32),
        ),
        in_specs=[vmem()] * 4,
        out_specs=(vmem(),) * 3,
        compiler_params=params(),
        name="finish",
    )(diagonal, terms, image, vector)


def after(value, *earlier):
    return lax.optimization_barrier((value, earlier))[0]


def swap_cores(part):
    return lax.ppermute(part, "col", [(i, i ^ 1) for i in range(32)])


def send_z(part):
    return lax.ppermute(part, "col", col_pairs(True))


def send_x(part):
    return lax.ppermute(part, "col", col_pairs(False))


def join(*parts):
    return jnp.concatenate([part if part.ndim == 3 else part[None] for part in parts], axis=0)


def per_device(blocks, block_row, block_col, counts, diagonal, vector):
    count = vector.shape[0] * lax.axis_size("row") * lax.axis_size("col")
    index = lax.axis_index("col")
    place = jnp.stack([index // 8, index // 2 % 4, index % 2]).astype(jnp.int32)
    partner_rows = swap_cores(block_row)
    diagonal = jnp.broadcast_to(diagonal[:, None], (2 * TILE, WIDTH))
    split = split_blocks(counts, blocks)
    slots = (place, block_row, block_col, split)

    def product(own):
        chip = join(swap_cores(own), own)
        z_chip = send_z(chip)
        x_chip = send_x(chip)
        z_chip = after(z_chip, x_chip, split, partner_rows)
        mid = join(z_chip, swap_cores(z_chip))
        z_far = send_z(z_chip[1])
        far_chip = send_x(x_chip[1])[None]
        x_mid = send_x(mid)
        last = join(swap_cores(z_far), z_far)
        x_last = send_x(last)
        x_mid = after(x_mid, last, far_chip)
        far_mid = send_x(x_mid[:2])
        far_last = send_x(x_last[1])[None]
        brought = (x_chip, x_mid, x_last, far_chip)
        other = swap_cores(pick_for_partner(early_brought, place, partner_rows, brought))
        sums = multiply_early(*slots, (chip, mid, last, *brought), other)
        brought = after((far_mid, far_last), sums)
        other = swap_cores(pick_for_partner(late_brought, place, partner_rows, brought))
        return lax.all_to_all(multiply_late(*slots, brought, other, *sums), "row", 0, 0, tiled=True)

    image = first_image(product(vector), diagonal, vector)
    return finish(count, diagonal, product(image), image, vector)


def solution(mesh):
    return jax.shard_map(
        per_device,
        mesh=mesh,
        in_specs=(
            P(("row", "col"), None, None),
            P(("row", "col")),
            P(("row", "col")),
            P(("row", "col")),
            P(("row", "col")),
            P(("row", "col"), None),
        ),
        out_specs=(P(("row", "col"), None), P(("row", "col"), None), P()),
        check_vma=False,
    )
```

```python
import functools

import jax
import jax.numpy as jnp
from jax import lax
from jax.experimental import pallas as pl
from jax.experimental.pallas import tpu as pltpu
from jax.sharding import PartitionSpec as P

TILE = 128
WIDTH = 256
STAT = 8
LIMIT = 48 * 1024 * 1024


def col_index(z, x, core):
    return (z % 4) * 8 + (x % 4) * 2 + core


def col_pairs(along_z):
    pairs = []
    for z in range(4):
        for x in range(4):
            for core, step in ((0, 1), (1, 3)):
                to = (z + step, x) if along_z else (z, x + step)
                pairs.append((col_index(z, x, core), col_index(*to, core)))
    return pairs


def smem():
    return pl.BlockSpec(memory_space=pltpu.SMEM)


def vmem():
    return pl.BlockSpec(memory_space=pltpu.VMEM)


def params():
    return pltpu.CompilerParams(vmem_limit_bytes=LIMIT)


def split_blocks_kernel(counts, blocks, out):
    base = pl.program_id(0) * blocks.shape[0]
    for i in range(blocks.shape[0]):
        block = jnp.where(base + i < counts[0], blocks[i], 0.0).T
        high = block.astype(jnp.bfloat16)
        low = (block - high.astype(jnp.float32)).astype(jnp.bfloat16)
        out[i, :, :TILE] = high
        out[i, :, TILE:] = low


def split_blocks(counts, blocks):
    n, step = blocks.shape[0], 8
    return pl.pallas_call(
        split_blocks_kernel,
        grid=(n // step,),
        out_shape=jax.ShapeDtypeStruct((n, TILE, 2 * TILE), jnp.bfloat16),
        in_specs=[smem(), pl.BlockSpec((step, TILE, TILE), lambda i: (i, 0, 0))],
        out_specs=pl.BlockSpec((step, TILE, 2 * TILE), lambda i: (i, 0, 0)),
        compiler_params=params(),
        name="split_blocks",
    )(counts, blocks)


NONE, WAY, AGAINST, TWO = range(4)
CHIP = ((NONE, 1), (NONE, 0))
MID = ((WAY, 1), (WAY, 0), (AGAINST, 0), (AGAINST, 1))
LAST = ((TWO, 1), (TWO, 0))


def named(dx, keys, ref):
    return [(dx, *key, ref, i) for i, key in enumerate(keys)]


def early_pieces(chip, mid, last):
    return named(NONE, CHIP, chip) + named(NONE, MID, mid) + named(NONE, LAST, last)


def early_brought(chip, mid, last, far):
    return named(WAY, CHIP, chip) + named(WAY, MID, mid) + named(WAY, LAST, last) + named(TWO, CHIP[1:], far)


def late_brought(mid, last):
    return named(TWO, MID[:2], mid) + named(TWO, LAST[1:], last)


def slot_of(place, dx, dz, other, core):
    steps = (0, 3 - 2 * core, 1 + 2 * core, 2)
    number = 1 - core if other else core
    return ((place[0] + steps[dz]) & 3) * 8 + ((place[1] + steps[dx]) & 3) * 2 + number


def pick_kernel(layout, place, rows, *refs):
    *brought, out = refs
    for n, (dx, dz, other, ref, i) in enumerate(layout(*brought)):
        slot = slot_of(place, dx, dz, other, place[2])
        start = pl.multiple_of((rows[slot] & 1) * TILE, TILE)
        out[n, :TILE] = ref[i, pl.ds(start, TILE)]
        if out.shape[1] > TILE:
            out[n, TILE:] = ref[i, 2 * TILE :]


def pick_for_partner(layout, place, partner_rows, brought):
    extra = brought[0].shape[1] - 2 * TILE
    return pl.pallas_call(
        functools.partial(pick_kernel, layout),
        out_shape=jax.ShapeDtypeStruct((len(layout(*brought)), TILE + extra, WIDTH), jnp.float32),
        in_specs=[smem(), smem()] + [vmem()] * len(brought),
        out_specs=vmem(),
        compiler_params=params(),
        name="pick_for_partner",
    )(place, partner_rows, *brought)


def merge(stats):
    squares, inner, rest = stats
    ratio = jnp.where(squares > 0, inner / jnp.where(squares > 0, squares, 1.0), 0.0)
    total, inner_total = jnp.sum(squares, axis=0), jnp.sum(inner, axis=0)
    safe = jnp.where(total > 0, total, 1.0)
    mean_ratio = jnp.where(total > 0, inner_total / safe, 0.0)
    away = ratio - mean_ratio[None]
    return total, inner_total, jnp.sum(rest + squares * away * away, axis=0), mean_ratio


def add_products(place, rows, cols, split, own, brought, other, out, stats):
    core = place[2]

    def add(slot, source):
        high = source.astype(jnp.bfloat16)
        low = (source - high.astype(jnp.float32)).astype(jnp.bfloat16)
        both = split[slot]
        total = jnp.dot(
            both, jnp.concatenate([high, high], axis=0), preferred_element_type=jnp.float32
        ) + jnp.dot(both, jnp.concatenate([low, low], axis=0), preferred_element_type=jnp.float32)
        target = cols[slot]
        owner = lax.shift_right_logical(target, 6)
        start = pl.multiple_of((target & 1) * TILE, TILE)
        out[owner, pl.ds(start, TILE)] += total

    for dx, dz, foreign, ref, i in own + brought:
        slot = slot_of(place, dx, dz, foreign, core)
        start = pl.multiple_of((rows[slot] & 1) * TILE, TILE)
        add(slot, ref[i, pl.ds(start, TILE)])
        if stats is not None:
            stats[slot] = ref[i, 2 * TILE :]
    for n, (dx, dz, foreign, _, _) in enumerate(brought):
        slot = slot_of(place, dx, dz, foreign, 1 - core)
        add(slot, other[n, :TILE])
        if stats is not None:
            stats[slot] = other[n, TILE:]


def early_kernel(place, rows, cols, split, *refs):
    out, stats = refs[8], refs[9] if len(refs) > 9 else None
    out[...] = jnp.zeros_like(out)
    if stats is not None:
        stats[...] = jnp.zeros_like(stats)
    own, brought = early_pieces(*refs[:3]), early_brought(*refs[3:7])
    add_products(place, rows, cols, split, own, brought, refs[7], out, stats)


def multiply_early(place, rows, cols, split, gathered, other):
    height = gathered[0].shape[1]
    shapes = [jax.ShapeDtypeStruct((8, height, WIDTH), jnp.float32)]
    if height > 2 * TILE:
        shapes.append(jax.ShapeDtypeStruct((32, STAT, WIDTH), jnp.float32))
    return pl.pallas_call(
        early_kernel,
        out_shape=shapes,
        in_specs=[smem()] * 3 + [vmem()] * (2 + len(gathered)),
        out_specs=[vmem()] * len(shapes),
        compiler_params=params(),
        name="multiply_early",
    )(place, rows, cols, split, *gathered, other)


def late_kernel(place, rows, cols, split, mid, last, other, sums, *refs):
    if len(refs) == 1:
        out, stats = refs[0], None
    else:
        known, out, stats = refs
        stats[...] = known[...]
    out[...] = sums[...]
    add_products(place, rows, cols, split, [], late_brought(mid, last), other, out, stats)
    if stats is not None:
        total, inner, rest, _ = merge([stats[:, k : k + 1, :] for k in range(3)])
        joined = jnp.concatenate([total, inner, rest, jnp.zeros((STAT - 3, WIDTH), jnp.float32)], axis=0)
        for owner in range(out.shape[0]):
            out[owner, 2 * TILE :] = joined


def multiply_late(place, rows, cols, split, gathered, other, sums, *stats):
    return pl.pallas_call(
        late_kernel,
        out_shape=jax.ShapeDtypeStruct(sums.shape, jnp.float32),
        in_specs=[smem()] * 3 + [vmem()] * (5 + len(stats)),
        out_specs=vmem(),
        scratch_shapes=[pltpu.VMEM(each.shape, jnp.float32) for each in stats],
        compiler_params=params(),
        name="multiply_late",
    )(place, rows, cols, split, *gathered, other, sums, *stats)


def sum_terms(terms, diagonal, source):
    total = terms[0, : 2 * TILE]
    for k in range(1, terms.shape[0]):
        total = total + terms[k, : 2 * TILE]
    return diagonal[...] * source + total


def first_image_kernel(terms, diagonal, vector, out):
    v = vector[...]
    w = sum_terms(terms, diagonal, v)
    out[: 2 * TILE] = w
    squares = jnp.sum(v * v, axis=0, keepdims=True)
    inner = jnp.sum(w * v, axis=0, keepdims=True)
    ratio = jnp.where(squares > 0, inner / jnp.where(squares > 0, squares, 1.0), 0.0)
    away = w - ratio * v
    rest = jnp.sum(away * away, axis=0, keepdims=True)
    out[2 * TILE :] = jnp.concatenate(
        [squares, inner, rest, jnp.zeros((STAT - 3, WIDTH), jnp.float32)], axis=0
    )


def first_image(terms, diagonal, vector):
    return pl.pallas_call(
        first_image_kernel,
        out_shape=jax.ShapeDtypeStruct((2 * TILE + STAT, WIDTH), jnp.float32),
        in_specs=[vmem()] * 3,
        out_specs=vmem(),
        compiler_params=params(),
        name="first_image",
    )(terms, diagonal, vector)


def finish_kernel(count, diagonal, terms, image, vector, basis, second, column):
    stats = [terms[:, 2 * TILE + k : 2 * TILE + k + 1, :] for k in range(3)]
    squares, inner, rest, ratio = merge(stats)
    mean = squares / count + 1e-06
    magnitude = jnp.sqrt(mean)
    projection = inner / count / mean
    gap = projection - ratio
    left_over = rest + squares * gap * gap
    norm = jnp.sqrt(left_over / count / mean + 1e-06)
    column[0:1] = projection
    column[1:2] = norm
    w = image[: 2 * TILE]
    scale = 1.0 / (magnitude * norm)
    basis[...] = (w - projection * vector[...]) * scale
    second[...] = (sum_terms(terms, diagonal, w) - projection * w) * scale


def finish(count, diagonal, terms, image, vector):
    return pl.pallas_call(
        functools.partial(finish_kernel, count),
        out_shape=(
            jax.ShapeDtypeStruct((2 * TILE, WIDTH), jnp.float32),
            jax.ShapeDtypeStruct((2 * TILE, WIDTH), jnp.float32),
            jax.ShapeDtypeStruct((2, WIDTH), jnp.float32),
        ),
        in_specs=[vmem()] * 4,
        out_specs=(vmem(),) * 3,
        compiler_params=params(),
        name="finish",
    )(diagonal, terms, image, vector)


def after(value, *earlier):
    return lax.optimization_barrier((value, earlier))[0]


def swap_cores(part):
    return lax.ppermute(part, "col", [(i, i ^ 1) for i in range(32)])


def send_z(part):
    return lax.ppermute(part, "col", col_pairs(True))


def send_x(part):
    return lax.ppermute(part, "col", col_pairs(False))


def join(*parts):
    return jnp.concatenate([part if part.ndim == 3 else part[None] for part in parts], axis=0)


def per_device(blocks, block_row, block_col, counts, diagonal, vector):
    count = vector.shape[0] * lax.axis_size("row") * lax.axis_size("col")
    index = lax.axis_index("col")
    place = jnp.stack([index // 8, index // 2 % 4, index % 2]).astype(jnp.int32)
    partner_rows = swap_cores(block_row)
    diagonal = jnp.broadcast_to(diagonal[:, None], (2 * TILE, WIDTH))
    split = split_blocks(counts, blocks)
    slots = (place, block_row, block_col, split)

    def product(own):
        other = swap_cores(own)
        z_own, z_other = send_z(own), send_z(other)
        chip = join(other, own)
        x_chip = send_x(chip)
        far_chip = send_x(x_chip[1])[None]
        z_chip = after(join(z_other, z_own), far_chip, split, partner_rows)
        mid = join(z_chip, swap_cores(z_chip))
        z_far = send_z(z_own)
        x_mid = send_x(mid)
        last = join(swap_cores(z_far), z_far)
        x_last = send_x(last)
        x_mid = after(x_mid, last)
        far_mid = send_x(x_mid[:2])
        far_last = send_x(x_last[1])[None]
        brought = (x_chip, x_mid, x_last, far_chip)
        other = swap_cores(pick_for_partner(early_brought, place, partner_rows, brought))
        sums = multiply_early(*slots, (chip, mid, last, *brought), other)
        brought = after((far_mid, far_last), sums)
        other = swap_cores(pick_for_partner(late_brought, place, partner_rows, brought))
        return lax.all_to_all(multiply_late(*slots, brought, other, *sums), "row", 0, 0, tiled=True)

    image = first_image(product(vector), diagonal, vector)
    return finish(count, diagonal, product(image), image, vector)


def solution(mesh):
    return jax.shard_map(
        per_device,
        mesh=mesh,
        in_specs=(
            P(("row", "col"), None, None),
            P(("row", "col")),
            P(("row", "col")),
            P(("row", "col")),
            P(("row", "col")),
            P(("row", "col"), None),
        ),
        out_specs=(P(("row", "col"), None), P(("row", "col"), None), P()),
        check_vma=False,
    )
```

```python
import functools

import jax
import jax.numpy as jnp
from jax import lax
from jax.experimental import pallas as pl
from jax.experimental.pallas import tpu as pltpu
from jax.sharding import PartitionSpec as P

TILE = 128
WIDTH = 256
STAT = 8
LIMIT = 48 * 1024 * 1024


def col_index(z, x, core):
    return (z % 4) * 8 + (x % 4) * 2 + core


def col_pairs(along_z):
    pairs = []
    for z in range(4):
        for x in range(4):
            for core, step in ((0, 1), (1, 3)):
                to = (z + step, x) if along_z else (z, x + step)
                pairs.append((col_index(z, x, core), col_index(*to, core)))
    return pairs


def smem():
    return pl.BlockSpec(memory_space=pltpu.SMEM)


def vmem():
    return pl.BlockSpec(memory_space=pltpu.VMEM)


def params():
    return pltpu.CompilerParams(vmem_limit_bytes=LIMIT)


def split_blocks_kernel(counts, blocks, out):
    base = pl.program_id(0) * blocks.shape[0]
    for i in range(blocks.shape[0]):
        block = jnp.where(base + i < counts[0], blocks[i], 0.0).T
        high = block.astype(jnp.bfloat16)
        low = (block - high.astype(jnp.float32)).astype(jnp.bfloat16)
        out[i, :, :TILE] = high
        out[i, :, TILE:] = low


def split_blocks(counts, blocks):
    n, step = blocks.shape[0], 8
    return pl.pallas_call(
        split_blocks_kernel,
        grid=(n // step,),
        out_shape=jax.ShapeDtypeStruct((n, TILE, 2 * TILE), jnp.bfloat16),
        in_specs=[smem(), pl.BlockSpec((step, TILE, TILE), lambda i: (i, 0, 0))],
        out_specs=pl.BlockSpec((step, TILE, 2 * TILE), lambda i: (i, 0, 0)),
        compiler_params=params(),
        name="split_blocks",
    )(counts, blocks)


NONE, WAY, AGAINST, TWO = range(4)
CHIP = ((NONE, 1), (NONE, 0))
MID = ((WAY, 1), (WAY, 0), (AGAINST, 0), (AGAINST, 1))
LAST = ((TWO, 1), (TWO, 0))


def named(dx, keys, ref):
    return [(dx, *key, ref, i) for i, key in enumerate(keys)]


def early_pieces(own, other, mid, last):
    return named(NONE, CHIP[1:], own) + named(NONE, CHIP[:1], other) + named(NONE, MID, mid) + named(NONE, LAST, last)


def early_brought(own, other, mid, last, far):
    return (
        named(WAY, CHIP[1:], own)
        + named(WAY, CHIP[:1], other)
        + named(WAY, MID, mid)
        + named(WAY, LAST, last)
        + named(TWO, CHIP[1:], far)
    )


def late_brought(mid, last):
    return named(TWO, MID[:2], mid) + named(TWO, LAST[1:], last)


def slot_of(place, dx, dz, other, core):
    steps = (0, 3 - 2 * core, 1 + 2 * core, 2)
    number = 1 - core if other else core
    return ((place[0] + steps[dz]) & 3) * 8 + ((place[1] + steps[dx]) & 3) * 2 + number


def pick_kernel(layout, place, rows, *refs):
    *brought, out = refs
    for n, (dx, dz, other, ref, i) in enumerate(layout(*brought)):
        slot = slot_of(place, dx, dz, other, place[2])
        start = pl.multiple_of((rows[slot] & 1) * TILE, TILE)
        out[n, :TILE] = ref[i, pl.ds(start, TILE)]
        if out.shape[1] > TILE:
            out[n, TILE:] = ref[i, 2 * TILE :]


def pick_for_partner(layout, place, partner_rows, brought):
    extra = brought[0].shape[1] - 2 * TILE
    return pl.pallas_call(
        functools.partial(pick_kernel, layout),
        out_shape=jax.ShapeDtypeStruct((len(layout(*brought)), TILE + extra, WIDTH), jnp.float32),
        in_specs=[smem(), smem()] + [vmem()] * len(brought),
        out_specs=vmem(),
        compiler_params=params(),
        name="pick_for_partner",
    )(place, partner_rows, *brought)


def merge(stats):
    squares, inner, rest = stats
    ratio = jnp.where(squares > 0, inner / jnp.where(squares > 0, squares, 1.0), 0.0)
    total, inner_total = jnp.sum(squares, axis=0), jnp.sum(inner, axis=0)
    safe = jnp.where(total > 0, total, 1.0)
    mean_ratio = jnp.where(total > 0, inner_total / safe, 0.0)
    away = ratio - mean_ratio[None]
    return total, inner_total, jnp.sum(rest + squares * away * away, axis=0), mean_ratio


def add_products(place, rows, cols, split, own, brought, other, out, stats):
    core = place[2]

    def add(slot, source):
        high = source.astype(jnp.bfloat16)
        low = (source - high.astype(jnp.float32)).astype(jnp.bfloat16)
        both = split[slot]
        total = jnp.dot(
            both, jnp.concatenate([high, high], axis=0), preferred_element_type=jnp.float32
        ) + jnp.dot(both, jnp.concatenate([low, low], axis=0), preferred_element_type=jnp.float32)
        target = cols[slot]
        owner = lax.shift_right_logical(target, 6)
        start = pl.multiple_of((target & 1) * TILE, TILE)
        out[owner, pl.ds(start, TILE)] += total

    for dx, dz, foreign, ref, i in own + brought:
        slot = slot_of(place, dx, dz, foreign, core)
        start = pl.multiple_of((rows[slot] & 1) * TILE, TILE)
        add(slot, ref[i, pl.ds(start, TILE)])
        if stats is not None:
            stats[slot] = ref[i, 2 * TILE :]
    for n, (dx, dz, foreign, _, _) in enumerate(brought):
        slot = slot_of(place, dx, dz, foreign, 1 - core)
        add(slot, other[n, :TILE])
        if stats is not None:
            stats[slot] = other[n, TILE:]


def early_kernel(place, rows, cols, split, *refs):
    out, stats = refs[10], refs[11] if len(refs) > 11 else None
    out[...] = jnp.zeros_like(out)
    if stats is not None:
        stats[...] = jnp.zeros_like(stats)
    own, brought = early_pieces(*refs[:4]), early_brought(*refs[4:9])
    add_products(place, rows, cols, split, own, brought, refs[9], out, stats)


def multiply_early(place, rows, cols, split, gathered, other):
    height = gathered[0].shape[1]
    shapes = [jax.ShapeDtypeStruct((8, height, WIDTH), jnp.float32)]
    if height > 2 * TILE:
        shapes.append(jax.ShapeDtypeStruct((32, STAT, WIDTH), jnp.float32))
    return pl.pallas_call(
        early_kernel,
        out_shape=shapes,
        in_specs=[smem()] * 3 + [vmem()] * (2 + len(gathered)),
        out_specs=[vmem()] * len(shapes),
        compiler_params=params(),
        name="multiply_early",
    )(place, rows, cols, split, *gathered, other)


def late_kernel(place, rows, cols, split, mid, last, other, sums, *refs):
    if len(refs) == 1:
        out, stats = refs[0], None
    else:
        known, out, stats = refs
        stats[...] = known[...]
    out[...] = sums[...]
    add_products(place, rows, cols, split, [], late_brought(mid, last), other, out, stats)
    if stats is not None:
        total, inner, rest, _ = merge([stats[:, k : k + 1, :] for k in range(3)])
        joined = jnp.concatenate([total, inner, rest, jnp.zeros((STAT - 3, WIDTH), jnp.float32)], axis=0)
        for owner in range(out.shape[0]):
            out[owner, 2 * TILE :] = joined


def multiply_late(place, rows, cols, split, gathered, other, sums, *stats):
    return pl.pallas_call(
        late_kernel,
        out_shape=jax.ShapeDtypeStruct(sums.shape, jnp.float32),
        in_specs=[smem()] * 3 + [vmem()] * (5 + len(stats)),
        out_specs=vmem(),
        scratch_shapes=[pltpu.VMEM(each.shape, jnp.float32) for each in stats],
        compiler_params=params(),
        name="multiply_late",
    )(place, rows, cols, split, *gathered, other, sums, *stats)


def sum_terms(terms, diagonal, source):
    total = terms[0, : 2 * TILE]
    for k in range(1, terms.shape[0]):
        total = total + terms[k, : 2 * TILE]
    return diagonal[...] * source + total


def first_image_kernel(terms, diagonal, vector, out):
    v = vector[...]
    w = sum_terms(terms, diagonal, v)
    out[: 2 * TILE] = w
    squares = jnp.sum(v * v, axis=0, keepdims=True)
    inner = jnp.sum(w * v, axis=0, keepdims=True)
    ratio = jnp.where(squares > 0, inner / jnp.where(squares > 0, squares, 1.0), 0.0)
    away = w - ratio * v
    rest = jnp.sum(away * away, axis=0, keepdims=True)
    out[2 * TILE :] = jnp.concatenate(
        [squares, inner, rest, jnp.zeros((STAT - 3, WIDTH), jnp.float32)], axis=0
    )


def first_image(terms, diagonal, vector):
    return pl.pallas_call(
        first_image_kernel,
        out_shape=jax.ShapeDtypeStruct((2 * TILE + STAT, WIDTH), jnp.float32),
        in_specs=[vmem()] * 3,
        out_specs=vmem(),
        compiler_params=params(),
        name="first_image",
    )(terms, diagonal, vector)


def finish_kernel(count, diagonal, terms, image, vector, basis, second, column):
    stats = [terms[:, 2 * TILE + k : 2 * TILE + k + 1, :] for k in range(3)]
    squares, inner, rest, ratio = merge(stats)
    mean = squares / count + 1e-06
    magnitude = jnp.sqrt(mean)
    projection = inner / count / mean
    gap = projection - ratio
    left_over = rest + squares * gap * gap
    norm = jnp.sqrt(left_over / count / mean + 1e-06)
    column[0:1] = projection
    column[1:2] = norm
    w = image[: 2 * TILE]
    scale = 1.0 / (magnitude * norm)
    basis[...] = (w - projection * vector[...]) * scale
    second[...] = (sum_terms(terms, diagonal, w) - projection * w) * scale


def finish(count, diagonal, terms, image, vector):
    return pl.pallas_call(
        functools.partial(finish_kernel, count),
        out_shape=(
            jax.ShapeDtypeStruct((2 * TILE, WIDTH), jnp.float32),
            jax.ShapeDtypeStruct((2 * TILE, WIDTH), jnp.float32),
            jax.ShapeDtypeStruct((2, WIDTH), jnp.float32),
        ),
        in_specs=[vmem()] * 4,
        out_specs=(vmem(),) * 3,
        compiler_params=params(),
        name="finish",
    )(diagonal, terms, image, vector)


def after(value, *earlier):
    return lax.optimization_barrier((value, earlier))[0]


def swap_cores(part):
    return lax.ppermute(part, "col", [(i, i ^ 1) for i in range(32)])


def send_z(part):
    return lax.ppermute(part, "col", col_pairs(True))


def send_x(part):
    return lax.ppermute(part, "col", col_pairs(False))


def join(*parts):
    return jnp.concatenate([part if part.ndim == 3 else part[None] for part in parts], axis=0)


def per_device(blocks, block_row, block_col, counts, diagonal, vector):
    count = vector.shape[0] * lax.axis_size("row") * lax.axis_size("col")
    index = lax.axis_index("col")
    place = jnp.stack([index // 8, index // 2 % 4, index % 2]).astype(jnp.int32)
    partner_rows = swap_cores(block_row)
    diagonal = jnp.broadcast_to(diagonal[:, None], (2 * TILE, WIDTH))
    split = split_blocks(counts, blocks)
    slots = (place, block_row, block_col, split)

    def product(own):
        other_own = swap_cores(own)
        z_own, z_other = send_z(own), send_z(other_own)
        x_own, x_other = send_x(own), send_x(other_own)
        far_own = send_x(x_own)
        z_chip = after(join(z_other, z_own), far_own, x_other, split, partner_rows)
        mid = join(z_chip, swap_cores(z_chip))
        z_far = send_z(z_own)
        x_mid = send_x(mid)
        last = join(swap_cores(z_far), z_far)
        x_last = send_x(last)
        x_mid = after(x_mid, last)
        far_mid = send_x(x_mid[:2])
        far_last = send_x(x_last[1])[None]
        brought = (x_own[None], x_other[None], x_mid, x_last, far_own[None])
        other = swap_cores(pick_for_partner(early_brought, place, partner_rows, brought))
        sums = multiply_early(*slots, (own[None], other_own[None], mid, last, *brought), other)
        brought = after((far_mid, far_last), sums)
        other = swap_cores(pick_for_partner(late_brought, place, partner_rows, brought))
        return lax.all_to_all(multiply_late(*slots, brought, other, *sums), "row", 0, 0, tiled=True)

    image = first_image(product(vector), diagonal, vector)
    return finish(count, diagonal, product(image), image, vector)


def solution(mesh):
    return jax.shard_map(
        per_device,
        mesh=mesh,
        in_specs=(
            P(("row", "col"), None, None),
            P(("row", "col")),
            P(("row", "col")),
            P(("row", "col")),
            P(("row", "col")),
            P(("row", "col"), None),
        ),
        out_specs=(P(("row", "col"), None), P(("row", "col"), None), P()),
        check_vma=False,
    )
```
